256 devices in a mesh: outer: 8 (over z_hi, x), inner: 32 (over z_lo, y, core).
Axes of the slice: x: 4, y: 4, z: 8 (z_hi: 2, z_lo: 4; z = z_hi * 4 + z_lo), core: 2. Of those that a mesh axis runs over, the one named last changes fastest.
Arguments:
- points: bfloat16 [16, 1048576], P(None, ('outer', 'inner')), may hold values from -3 to 3
- charges: bfloat16 [64, 1048576], P(None, ('outer', 'inner')), may hold values from -6 to 6
- near_leaves: int32 [4096, 16], P(('outer', 'inner')), may hold values from 0 to 4095, as said below
- skel_device: int32 [256, 512], P(('outer', 'inner')), may hold values from 0 to 4095, as said below
- skel_tree: int32 [256, 7, 512], P(('outer', 'inner')), may hold values from 0 to 1023, as said below
Outputs:
- potential: float32 [64, 1048576], P(None, ('outer', 'inner'))
The draws below stay inside these ranges and needn't reach their ends.
Inputs may be any that keep to these rules, and one draw needn't show every extreme that they name: `near_leaves`: row b holds 16 different leaf numbers, b among them, each a leaf of b's level-0 node or of the level-0 nodes just before and just after it. `skel_device`: row c holds 512 different offsets among the 4096 points of level-0 node c. skel_tree[c, k] holds 512 different positions among the 1024 skeleton points of the children of the level-(k+1) node that contains level-0 node c; all level-0 nodes inside one level-(k+1) node have equal rows k.
All inputs are finite; a program needn't handle non-finite values.
Results may differ from the reference program's by a relative error of at most 0.0035.
Values may be sent and summed in bfloat16 or wider, within the bound.
No kernel may reach another device: no remote copies, remote signals or barrier semaphores. Data moves between devices by JAX's collectives and lax.ppermute only.
A program may use at most 64 MiB of HBM per device.

```python
import jax
import jax.numpy as jnp
from jax import lax

DIM = 16
NRHS = 64
LEAF = 256
R = 512
NNEAR = 16
LEAF_DEV = 16
NODES = 256
NDEV = 4096
NLEAVES = 4096
NPTS = 1048576
LEVELS = 8


def draw_points(key, part):

    def unit_terms(salt, count):
        sub_key = jax.random.fold_in(key, salt)
        return jnp.clip(jax.random.normal(sub_key, (DIM, count), jnp.float32), -4.0, 4.0)
    total = 0.53 * unit_terms(1, NPTS)
    total = total + 0.32 * jnp.repeat(unit_terms(2, NLEAVES), LEAF, axis=1)
    for height in range(LEVELS):
        groups = NODES >> height
        factor = 0.6 if height == 0 else 0.38
        total = total + factor * jnp.repeat(unit_terms(3 + height, groups), NPTS // groups, axis=1)
    return jnp.clip(total, -3.0, 3.0).astype(jnp.bfloat16)


def draw_near_leaves(key, part):
    window = 3 * LEAF_DEV
    leaf_ids = jnp.arange(NLEAVES, dtype=jnp.int32)
    offsets = jnp.arange(window, dtype=jnp.int32)
    first = (leaf_ids // LEAF_DEV - 1) * LEAF_DEV
    candidate = first[:, None] + offsets[None, :]
    inside = (candidate >= 0) & (candidate < NLEAVES)
    scores = jax.random.randint(key, (NLEAVES, window), 0, 2 ** 20, dtype=jnp.int32) * window + offsets[None, :]
    scores = jnp.where(candidate == leaf_ids[:, None], 2 ** 30, scores)
    scores = jnp.where(inside, scores, -1)
    ranked, picked = lax.top_k(scores, NNEAR)
    return jnp.take_along_axis(candidate, picked, axis=1).astype(jnp.int32)


def draw_skel_device(key, part):

    def one_node(node_id):
        return jax.random.permutation(jax.random.fold_in(key, node_id), NDEV)[:R]
    return jax.vmap(one_node)(jnp.arange(NODES, dtype=jnp.int32)).astype(jnp.int32)


def draw_skel_tree(key, part):
    base_key = jax.random.fold_in(key, 91)
    layers = []
    for height in range(LEVELS - 1):
        groups = NODES >> height + 1
        layer_key = jax.random.fold_in(base_key, height)

        def one_group(group_id):
            return jax.random.permutation(jax.random.fold_in(layer_key, group_id), 2 * R)[:R]
        chosen = jax.vmap(one_group)(jnp.arange(groups, dtype=jnp.int32))
        layers.append(jnp.repeat(chosen, 2 ** (height + 1), axis=0))
    return jnp.stack(layers, axis=1).astype(jnp.int32)


def block_levels(own_key, extent, split, low, largest):
    def one(position, blocks):
        draws = jax.random.uniform(jax.random.fold_in(jax.random.fold_in(own_key, 6), position), (blocks,), jnp.float32, low / len(split), largest / len(split))
        return jnp.repeat(jnp.exp(draws), extent[position] // blocks).reshape((-1,) + (1,) * (len(extent) - position - 1))

    loudness = one(*split[0])
    for cut in split[1:]:
        loudness = loudness * one(*cut)
    return loudness


def normal_values(own_key, dims, deviation, reach, cuts=(), held_as=jnp.bfloat16):
    drawn = jax.random.normal(own_key, dims, jnp.float32) * deviation
    if len(cuts) > 0:
        drawn = block_levels(own_key, dims, cuts, -0.22, 0.18) * drawn
    return jnp.clip(drawn, min=-reach, max=reach).astype(held_as)


def setup_inputs(seed: int = 0) -> dict:
    splits = jax.random.split(jax.random.key(seed), 6)
    return {
        "points": draw_points(jax.random.fold_in(splits[5], 71), 0),
        "charges": normal_values(splits[1], (NRHS, NPTS), 1.0, 6.0, ((1, 256),)),
        "near_leaves": draw_near_leaves(jax.random.fold_in(splits[5], 71), 0),
        "skel_device": draw_skel_device(jax.random.fold_in(splits[5], 71), 0),
        "skel_tree": draw_skel_tree(jax.random.fold_in(splits[5], 71), 0),
    }


GAMMA = 0.125


def kernel_block(left, right):
    left32 = left.astype(jnp.float32)
    right32 = right.astype(jnp.float32)
    products = jnp.einsum("dm,dn->mn", left32, right32, precision=lax.Precision.HIGHEST)
    distance = jnp.sum(left32 * left32, 0)[:, None] + jnp.sum(right32 * right32, 0)[None, :] - 2.0 * products
    return jnp.exp(-GAMMA * distance).astype(jnp.bfloat16)


def spread_weights(weights, block):
    totals = jnp.sum(block.astype(jnp.float32), 1)
    return (weights.astype(jnp.float32) / totals[None, :]).astype(jnp.bfloat16)


def carry_values(values, block):
    totals = jnp.sum(block.astype(jnp.float32), 0)
    return jnp.dot(values, block, preferred_element_type=jnp.float32) / totals[None, :]


def parent_node(joined, chosen):
    joined_x = joined[:DIM]
    parent_x = jnp.take(joined_x, chosen, axis=1)
    block = kernel_block(joined_x, parent_x)
    parent_up = jnp.dot(spread_weights(joined[DIM:], block), block, preferred_element_type=jnp.float32).astype(jnp.bfloat16)
    return jnp.concatenate([parent_x, parent_up], 0)


def downward_top(sibling, own_x):
    return jnp.dot(sibling[DIM:], kernel_block(sibling[:DIM], own_x), preferred_element_type=jnp.float32).astype(jnp.bfloat16)


def downward_node(sibling, parent_x, parent_down, own_x):
    beside = jnp.dot(sibling[DIM:], kernel_block(sibling[:DIM], own_x), preferred_element_type=jnp.float32)
    above = carry_values(parent_down, kernel_block(parent_x, own_x))
    return (beside + above).astype(jnp.bfloat16)


def near_block(leaves, targets_x, leaf_ids):
    target32 = targets_x.astype(jnp.float32)
    target_norm = jnp.sum(target32 * target32, 1)

    def one_turn(turn, summed):
        source = jnp.take(leaves, leaf_ids[:, turn], axis=0)
        source32 = source[:, :DIM].astype(jnp.float32)
        products = jnp.einsum("bdt,bds->bts", target32, source32, precision=lax.Precision.HIGHEST)
        distance = target_norm[:, :, None] + jnp.sum(source32 * source32, 1)[:, None, :] - 2.0 * products
        weights = jnp.exp(-GAMMA * distance).astype(jnp.bfloat16)
        return summed + jnp.einsum("bts,brs->rbt", weights.astype(jnp.float32), source[:, DIM:].astype(jnp.float32), precision=lax.Precision.HIGHEST)

    start = jnp.zeros((NRHS, targets_x.shape[0], targets_x.shape[2]), jnp.float32)
    return lax.fori_loop(0, leaf_ids.shape[1], one_turn, start)


def reference(points, charges, near_leaves, skel_device, skel_tree):
    nodes = skel_device.shape[0]
    levels = skel_tree.shape[1] + 1
    dev_points = points.shape[1] // nodes
    coords = points.reshape(DIM, nodes, dev_points).transpose(1, 0, 2)
    loads = charges.reshape(NRHS, nodes, dev_points).transpose(1, 0, 2)

    def leaf_up(inputs):
        node_x, node_q, chosen = inputs
        base_x = jnp.take(node_x, chosen, axis=1)
        block = kernel_block(node_x, base_x)
        base_up = jnp.dot(spread_weights(node_q, block), block, preferred_element_type=jnp.float32).astype(jnp.bfloat16)
        return jnp.concatenate([base_x, base_up], 0)

    level_nodes = [lax.map(leaf_up, (coords, loads, skel_device))]
    for height in range(levels - 1):
        current = level_nodes[-1]
        joined = jnp.concatenate([current[0::2], current[1::2]], 2)
        chosen = skel_tree[0::2 ** (height + 1), height]
        level_nodes.append(lax.map(lambda inputs: parent_node(inputs[0], inputs[1]), (joined, chosen)))

    downward = None
    for height in range(levels - 1, -1, -1):
        current = level_nodes[height]
        number = current.shape[0]
        sibling = current.reshape(number // 2, 2, DIM + NRHS, R)[:, ::-1].reshape(number, DIM + NRHS, R)
        if height == levels - 1:
            downward = lax.map(lambda inputs: downward_top(inputs[0], inputs[1][:DIM]), (sibling, current))
        else:
            parent_x = jnp.repeat(level_nodes[height + 1][:, :DIM], 2, axis=0)
            parent_down = jnp.repeat(downward, 2, axis=0)
            downward = lax.map(lambda inputs: downward_node(inputs[0], inputs[1], inputs[2], inputs[3][:DIM]), (sibling, parent_x, parent_down, current))

    base_x = level_nodes[0][:, :DIM]

    def far_field(inputs):
        node_down, node_base, node_x = inputs
        return carry_values(node_down, kernel_block(node_base, node_x))

    far_part = lax.map(far_field, (downward, base_x, coords))

    stacked = jnp.concatenate([points, charges], 0)
    leaves = stacked.reshape(DIM + NRHS, nodes * LEAF_DEV, LEAF).transpose(1, 0, 2)
    id_blocks = near_leaves.reshape(nodes, LEAF_DEV, NNEAR)

    def near_node(inputs):
        node_id, leaf_ids = inputs
        targets = lax.dynamic_slice_in_dim(leaves, (node_id * LEAF_DEV).astype(jnp.int32), LEAF_DEV, 0)
        return near_block(leaves, targets[:, :DIM], leaf_ids).reshape(NRHS, LEAF_DEV * LEAF)

    near_part = lax.map(near_node, (jnp.arange(nodes, dtype=jnp.int32), id_blocks))
    total = near_part + far_part
    return total.transpose(1, 0, 2).reshape(NRHS, nodes * dev_points)
```

```python
import functools
import math

import jax
import jax.numpy as jnp
from jax import lax
from jax.experimental import pallas as pl
from jax.experimental.pallas import tpu as pltpu
from jax.sharding import PartitionSpec as P

DIM = 16
NRHS = 64
LEAF = 256
TILE = 128
DEPTH = 32
ROWS = 96
GAMMA = 0.125
F32 = jnp.float32
BF16 = jnp.bfloat16

LOG2E = 1.0 / math.log(2.0)
VMEM_LIMIT = 24 * 2**20


def split_rows(x):
    wide = x.astype(F32)
    rest = (-GAMMA) * jnp.sum(wide * wide, axis=0, keepdims=True)
    row = lax.broadcasted_iota(jnp.int32, (DIM, x.shape[1]), 0)
    terms = jnp.where((row >= 3) & (row < 6), 1.0, 0.0)
    for i in range(3):
        term = rest.astype(BF16).astype(F32)
        rest = rest - term
        terms = jnp.where(row == i, term, terms)
    return wide, row, terms


def left_rows(x):
    wide, row, terms = split_rows(x)
    return jnp.concatenate([wide, terms], 0).astype(BF16).T


def right_rows(x):
    wide, row, terms = split_rows(x)
    turned = jnp.where(row < 3, 1.0, 0.0)
    for i in range(3):
        turned = jnp.where(row == i + 3, terms[i : i + 1], turned)
    return jnp.concatenate([wide * (2.0 * GAMMA), turned], 0).astype(BF16)


def dot(a, b):
    return jnp.dot(a, b, preferred_element_type=F32)


def dot_nt(a, b):
    return lax.dot_general(a, b, (((1,), (1,)), ((), ())), preferred_element_type=F32)


def entries(left, right):
    return jnp.exp2(dot(left, right) * LOG2E)


def pick(tiles, index):
    out = []
    for at in range(0, index.shape[1], TILE):
        here = jnp.broadcast_to(index[:, at : at + TILE], (DIM, TILE))
        lane = here & (TILE - 1)
        which = here >> 7
        got = jnp.zeros((DIM, TILE), F32)
        for number, tile in enumerate(tiles):
            got = jnp.where(which == number, jnp.take_along_axis(tile, lane, axis=1), got)
        out.append(got)
    return jnp.concatenate(out, 1)


def tiles_of(x):
    x = x.astype(F32)
    return [x[:, at : at + TILE] for at in range(0, x.shape[1], TILE)]


def index_rows(index):
    row = lax.broadcasted_iota(jnp.int32, (16, index.shape[1]), 0)
    high = (index >> 5).astype(F32)
    low = (index & 31).astype(F32)
    return jnp.where(row == 0, high, jnp.where(row == 1, low, 0.0))


def index_of(rows):
    rows = rows.astype(F32)
    return (rows[0:1] * 32.0 + rows[1:2]).astype(jnp.int32)


def base_kernel(points, charges, chosen, tree, node, block, inverse):
    base_x = pick(
        [points[:, at : at + TILE].astype(F32) for at in range(0, points.shape[1], TILE)],
        chosen[...],
    )
    left = left_rows(base_x)
    count = base_x.shape[1]
    up = jnp.zeros((NRHS, count), F32)
    for at in range(0, points.shape[1], LEAF):
        right = right_rows(points[:, at : at + LEAF])
        total = jnp.zeros((1, LEAF), F32)
        for top in range(0, count, LEAF):
            piece = entries(left[top : top + LEAF], right)
            total = total + jnp.sum(piece, axis=0, keepdims=True)
            block[top : top + LEAF, at : at + LEAF] = piece.astype(BF16)
        scale = 1.0 / total
        inverse[:, at : at + LEAF] = scale
        weights = (charges[:, at : at + LEAF].astype(F32) * scale).astype(BF16)
        up = up + dot_nt(weights, block[:, at : at + LEAF])
    node[0:DIM] = base_x.astype(BF16)
    node[DIM : DIM + NRHS] = up.astype(BF16)
    node[DIM + NRHS : ROWS] = index_rows(tree[0:1]).astype(BF16)


def call(kernel, outs, args, name, scratch=(), smem=(), flops=0):
    specs = [
        pl.BlockSpec(memory_space=pltpu.SMEM if i in smem else pltpu.VMEM)
        for i in range(len(args))
    ]
    moved = sum(a.size * a.dtype.itemsize for a in args)
    return pl.pallas_call(
        kernel,
        out_shape=[jax.ShapeDtypeStruct(s, t) for s, t in outs],
        in_specs=specs,
        out_specs=[pl.BlockSpec(memory_space=pltpu.VMEM)] * len(outs),
        scratch_shapes=list(scratch),
        compiler_params=pltpu.CompilerParams(vmem_limit_bytes=VMEM_LIMIT),
        cost_estimate=pl.CostEstimate(flops=flops, bytes_accessed=moved, transcendentals=0),
        name=name,
    )(*args)


def source_kernel(before_x, own_x, after_x, before_q, own_q, after_q, lefts, rights, loads):
    leaves = own_x.shape[1] // LEAF
    for part, (x, q) in enumerate(((before_x, before_q), (own_x, own_q), (after_x, after_q))):
        for leaf in range(leaves):
            at = leaf * LEAF
            here = x[:, at : at + LEAF]
            lefts[part * leaves + leaf] = left_rows(here)
            loads[part * leaves + leaf] = q[:, at : at + LEAF]
            if part == 1:
                rights[leaf] = right_rows(here)


def near_part(start, count, shift, ids, lefts, rights, loads, out, held):
    turns = ids.shape[1]

    def fill(leaf, turn):
        source = ids[start + leaf, turn] - shift
        held[turn] = entries(lefts[source], rights[start + leaf]).astype(BF16)

    def use(leaf, turn, summed):
        source = ids[start + leaf, turn] - shift
        return summed + dot(loads[source], held[turn])

    for turn in range(turns):
        fill(0, turn)

    def step(leaf, carry):
        summed = jnp.zeros((NRHS, LEAF), F32)
        for turn in range(turns):
            summed = use(leaf - 1, turn, summed)
            fill(leaf, turn)
        out[leaf - 1] = summed
        return carry

    lax.fori_loop(1, count, step, 0)
    summed = jnp.zeros((NRHS, LEAF), F32)
    for turn in range(turns):
        summed = use(count - 1, turn, summed)
    out[count - 1] = summed


def beside(source, target_x, held, out):
    left = left_rows(source[0:DIM])
    right = right_rows(target_x)
    count = target_x.shape[1]
    for top in range(0, count, LEAF):
        for at in range(0, count, LEAF):
            held[top : top + LEAF, at : at + LEAF] = entries(
                left[top : top + LEAF], right[:, at : at + LEAF]
            ).astype(BF16)
    out[...] = dot(source[DIM : DIM + NRHS], held[...])


def near_kernel(start, count, with_sides, where, ids, *refs):
    shift = (where[0] - 1) * (ids.shape[0])
    lefts, rights, loads = refs[:3]
    refs = refs[3:]
    if with_sides:
        own, sibling, parent, uncle, out, side_low, side_high, held, square = refs
        beside(sibling, own[0:DIM], square, side_low)
        beside(uncle, parent[0:DIM], square, side_high)
    else:
        out, held = refs
    near_part(start, count, shift, ids, lefts, rights, loads, out, held)


def link(parent_left, child_x, block, inverse):
    right = right_rows(child_x)
    count = child_x.shape[1]
    for at in range(0, count, LEAF):
        total = jnp.zeros((1, LEAF), F32)
        for top in range(0, count, LEAF):
            piece = entries(parent_left[top : top + LEAF], right[:, at : at + LEAF])
            total = total + jnp.sum(piece, axis=0, keepdims=True)
            block[top : top + LEAF, at : at + LEAF] = piece.astype(BF16)
        inverse[:, at : at + LEAF] = 1.0 / total


def lifted(charges, block, inverse):
    weights = (charges.astype(F32) * inverse[...]).astype(BF16)
    return dot_nt(weights, block[...])


def climb_kernel(low, where, tree, own, sibling, cousin, far_cousin, node, parent, uncle,
                 block_low, inverse_low, block_high, inverse_high, square, spare):
    bit_low = ((where[0] >> low) & 1) * 512
    bit_high = ((where[0] >> (low + 1)) & 1) * 512
    parent_x = pick(tiles_of(own[0:DIM]) + tiles_of(sibling[0:DIM]), tree[low : low + 1] ^ bit_low)
    uncle_x = pick(
        tiles_of(cousin[0:DIM]) + tiles_of(far_cousin[0:DIM]),
        index_of(cousin[DIM + NRHS : ROWS]) ^ bit_low,
    )
    next_x = pick(tiles_of(parent_x) + tiles_of(uncle_x), tree[low + 1 : low + 2] ^ bit_high)
    left = left_rows(parent_x)
    link(left, own[0:DIM], block_low, inverse_low)
    link(left, sibling[0:DIM], square, spare)
    up_parent = lifted(own[DIM : DIM + NRHS], block_low, inverse_low) + lifted(
        sibling[DIM : DIM + NRHS], square, spare
    )
    up_parent = up_parent.astype(BF16)
    left = left_rows(uncle_x)
    link(left, cousin[0:DIM], square, spare)
    up_uncle = lifted(cousin[DIM : DIM + NRHS], square, spare)
    link(left, far_cousin[0:DIM], square, spare)
    up_uncle = up_uncle + lifted(far_cousin[DIM : DIM + NRHS], square, spare)
    up_uncle = up_uncle.astype(BF16)
    left = left_rows(next_x)
    link(left, parent_x, block_high, inverse_high)
    link(left, uncle_x, square, spare)
    up_next = lifted(up_parent, block_high, inverse_high) + lifted(up_uncle, square, spare)
    node[0:DIM] = next_x.astype(BF16)
    node[DIM : DIM + NRHS] = up_next.astype(BF16)
    node[DIM + NRHS : ROWS] = index_rows(tree[low + 2 : low + 3]).astype(BF16)
    parent[0:DIM] = parent_x.astype(BF16)
    parent[DIM:] = up_parent
    uncle[0:DIM] = uncle_x.astype(BF16)
    uncle[DIM:] = up_uncle


def down_kernel(low, where, tree, own, sibling, cousin, far_cousin, *refs):
    levels = low
    blocks = refs[0 : 3 * levels]
    base_block, base_inverse = refs[3 * levels : 3 * levels + 2]
    rest = refs[3 * levels + 2 :]
    nears, (out, square, spare, side, top_block, top_inverse, uncle) = rest[:-7], rest[-7:]
    bit_low = ((where[0] >> low) & 1) * 512
    parent_x = pick(tiles_of(own[0:DIM]) + tiles_of(sibling[0:DIM]), tree[low : low + 1] ^ bit_low)
    uncle_x = pick(
        tiles_of(cousin[0:DIM]) + tiles_of(far_cousin[0:DIM]),
        index_of(cousin[DIM + NRHS : ROWS]) ^ bit_low,
    )
    link(left_rows(parent_x), own[0:DIM], top_block, top_inverse)
    left = left_rows(uncle_x)
    link(left, cousin[0:DIM], square, spare)
    up_uncle = lifted(cousin[DIM : DIM + NRHS], square, spare)
    link(left, far_cousin[0:DIM], square, spare)
    up_uncle = up_uncle + lifted(far_cousin[DIM : DIM + NRHS], square, spare)
    uncle[0:DIM] = uncle_x.astype(BF16)
    uncle[DIM:] = up_uncle.astype(BF16)
    beside(uncle, parent_x, square, side)
    downward = side[...].astype(BF16)
    beside(sibling, own[0:DIM], square, side)
    downward = (side[...] + dot(downward, top_block[...]) * top_inverse[...]).astype(BF16)
    for level in range(levels - 1, -1, -1):
        block, inverse, across = blocks[3 * level : 3 * level + 3]
        downward = (across[...] + dot(downward, block[...]) * inverse[...]).astype(BF16)
    at = 0
    for near in nears:
        for leaf in range(near.shape[0]):
            here = slice(at, at + LEAF)
            out[:, here] = near[leaf] + dot(downward, base_block[:, here]) * base_inverse[:, here]
            at += LEAF


def swapped(array, bits, inner_levels):
    inner, outer = lax.axis_size("inner"), lax.axis_size("outer")
    total = inner * outer
    mask = sum(1 << b for b in bits)
    return lax.ppermute(array, ("outer", "inner"), [(i, i ^ mask) for i in range(total)])


def body(points, charges, near_leaves, skel_device, skel_tree):
    inner_levels = lax.axis_size("inner").bit_length() - 1
    outer_levels = lax.axis_size("outer").bit_length() - 1
    levels = inner_levels + outer_levels
    total = 1 << levels
    position = lax.axis_index(("outer", "inner"))
    where = position.astype(jnp.int32).reshape(1)
    width = points.shape[1]
    leaves = near_leaves.shape[0]
    count = skel_device.shape[1]
    tree = skel_tree[0]
    ring = ("outer", "inner")
    ahead = [(i, (i + 1) % total) for i in range(total)]
    back = [((i + 1) % total, i) for i in range(total)]
    before_x = lax.ppermute(points, ring, ahead)
    after_x = lax.ppermute(points, ring, back)
    before_q = lax.ppermute(charges, ring, ahead)
    after_q = lax.ppermute(charges, ring, back)

    square = pltpu.VMEM((count, count), BF16)
    line = pltpu.VMEM((1, count), F32)
    side_out = ((NRHS, count), F32)
    node_out = ((ROWS, count), BF16)
    pair_out = ((DIM + NRHS, count), BF16)
    block_out = [((count, count), BF16), ((1, count), F32)]

    node, base_block, base_inverse = call(
        base_kernel,
        [node_out, ((count, width), BF16), ((1, width), F32)],
        (points, charges, skel_device, tree),
        "base",
        flops=2 * width * count * (DEPTH + NRHS),
    )
    rounds = levels // 2
    chunk = leaves // rounds
    records = {}
    nears = []
    pending = None
    sources = None
    for turn in range(rounds):
        low = 2 * turn
        sibling = swapped(node, (low,), inner_levels)
        cousin = swapped(node, (low + 1,), inner_levels)
        far_cousin = swapped(node, (low, low + 1), inner_levels)
        if sources is None:
            sources = call(
                source_kernel,
                [
                    ((3 * leaves, LEAF, DEPTH), BF16),
                    ((leaves, DEPTH, LEAF), BF16),
                    ((3 * leaves, NRHS, LEAF), BF16),
                ],
                (before_x, points, after_x, before_q, charges, after_q),
                "sources",
                flops=10**9,
            )
        sources, node = lax.optimization_barrier((sources, node))
        args = (where, near_leaves, *sources)
        outs = [((chunk, NRHS, LEAF), F32)]
        scratch = [pltpu.VMEM((near_leaves.shape[1], LEAF, LEAF), BF16)]
        if pending is not None:
            args += pending
            outs += [side_out, side_out]
            scratch.append(square)
        made = call(
            functools.partial(near_kernel, turn * chunk, chunk, pending is not None),
            outs,
            args,
            "near",
            scratch,
            smem=(0, 1),
            flops=2 * chunk * LEAF * near_leaves.shape[1] * LEAF * (DEPTH + NRHS),
        )
        part, sibling, cousin, far_cousin = lax.optimization_barrier((made[0], sibling, cousin, far_cousin))
        nears.append(part)
        if pending is not None:
            records[low - 2].append(made[1])
            records[low - 1].append(made[2])
        if turn < rounds - 1:
            following, parent, uncle, block_low, inverse_low, block_high, inverse_high = call(
                functools.partial(climb_kernel, low),
                [node_out, pair_out, pair_out, *block_out, *block_out],
                (where, tree, node, sibling, cousin, far_cousin),
                "climb",
                [square, line],
                smem=(0,),
                flops=6 * 2 * count * count * (DEPTH + NRHS),
            )
            records[low] = [block_low, inverse_low]
            records[low + 1] = [block_high, inverse_high]
            pending = (node, sibling, parent, uncle)
            node = following
    low = levels - 2
    kept = [array for level in range(low) for array in records[level]]
    [potential] = call(
        functools.partial(down_kernel, low),
        [((NRHS, width), F32)],
        (where, tree, node, sibling, cousin, far_cousin, *kept, base_block, base_inverse, *nears),
        "down",
        [square, line, pltpu.VMEM(*side_out), square, line, pltpu.VMEM(*pair_out)],
        smem=(0,),
        flops=2 * width * count * NRHS,
    )
    return potential


def solution(mesh):
    return jax.shard_map(
        body,
        mesh=mesh,
        in_specs=(
            P(None, ("outer", "inner")),
            P(None, ("outer", "inner")),
            P(("outer", "inner"), None),
            P(("outer", "inner"), None),
            P(("outer", "inner"), None, None),
        ),
        out_specs=P(None, ("outer", "inner")),
        check_vma=False,
    )
```

```python
import functools
import math

import jax
import jax.numpy as jnp
from jax import lax
from jax.experimental import pallas as pl
from jax.experimental.pallas import tpu as pltpu
from jax.sharding import PartitionSpec as P

DIM = 16
NRHS = 64
LEAF = 256
TILE = 128
DEPTH = 32
GAMMA = 0.125
F32 = jnp.float32
BF16 = jnp.bfloat16

LOG2E = 1.0 / math.log(2.0)
VMEM_LIMIT = 24 * 2**20


def split_rows(x):
    wide = x.astype(F32)
    rest = (-GAMMA) * jnp.sum(wide * wide, axis=0, keepdims=True)
    row = lax.broadcasted_iota(jnp.int32, (DIM, x.shape[1]), 0)
    terms = jnp.where((row >= 3) & (row < 6), 1.0, 0.0)
    for i in range(3):
        term = rest.astype(BF16).astype(F32)
        rest = rest - term
        terms = jnp.where(row == i, term, terms)
    return wide, row, terms


def left_rows(x):
    wide, row, terms = split_rows(x)
    return jnp.concatenate([wide, terms], 0).astype(BF16).T


def right_rows(x):
    wide, row, terms = split_rows(x)
    turned = jnp.where(row < 3, 1.0, 0.0)
    for i in range(3):
        turned = jnp.where(row == i + 3, terms[i : i + 1], turned)
    return jnp.concatenate([wide * (2.0 * GAMMA), turned], 0).astype(BF16)


def dot(a, b):
    return jnp.dot(a, b, preferred_element_type=F32)


def dot_nt(a, b):
    return lax.dot_general(a, b, (((1,), (1,)), ((), ())), preferred_element_type=F32)


def entries(left, right):
    return jnp.exp2(dot(left, right) * LOG2E)


def pick(tiles, index):
    out = []
    for at in range(0, index.shape[1], TILE):
        here = jnp.broadcast_to(index[:, at : at + TILE], (DIM, TILE))
        lane = here & (TILE - 1)
        which = here >> 7
        got = jnp.zeros((DIM, TILE), F32)
        for number, tile in enumerate(tiles):
            got = jnp.where(which == number, jnp.take_along_axis(tile, lane, axis=1), got)
        out.append(got)
    return jnp.concatenate(out, 1)


def tiles_of(x):
    x = x.astype(F32)
    return [x[:, at : at + TILE] for at in range(0, x.shape[1], TILE)]


def base_kernel(
    points_in, charges_in, tree_in, chosen_in, ids_in,
    node, block, inverse, points, charges, rights, tree_out, ids,
    tree, chosen, sems,
):
    position = lax.axis_index(("outer", "inner"))
    copies = [
        pltpu.make_async_copy(source, target, sems.at[i])
        for i, (source, target) in enumerate(
            (
                (points_in, points),
                (chosen_in, chosen),
                (tree_in, tree),
                (charges_in, charges),
                (ids_in, ids),
            )
        )
    ]
    for copy in copies:
        copy.start()
    leaves = rights.shape[0]
    copies[0].wait()
    copies[1].wait()
    base_x = pick(
        [points[:, at : at + TILE].astype(F32) for at in range(0, points.shape[1], TILE)],
        chosen[...],
    )
    node[0:DIM] = base_x.astype(BF16)
    left = left_rows(base_x)
    count = base_x.shape[1]
    copies[2].wait()
    for level in range(tree.shape[0]):
        bit = ((position >> level) & 1) * count
        tree_out[level : level + 1] = tree[level] ^ bit
    copies[3].wait()
    up = jnp.zeros((NRHS, count), F32)
    for leaf in range(leaves):
        here = slice(leaf * LEAF, (leaf + 1) * LEAF)
        right = right_rows(points[:, here])
        rights[leaf] = right
        total = jnp.zeros((1, LEAF), F32)
        for top in range(0, count, LEAF):
            piece = entries(left[top : top + LEAF], right)
            total = total + jnp.sum(piece, axis=0, keepdims=True)
            block[top : top + LEAF, here] = piece.astype(BF16)
        scale = 1.0 / total
        inverse[:, here] = scale
        weights = (charges[:, here].astype(F32) * scale).astype(BF16)
        up = up + dot_nt(weights, block[:, here])
    node[DIM:] = up.astype(BF16)
    copies[4].wait()


def call(kernel, outs, args, name, scratch=(), spaces={}, out_spaces={}, aliases={}, flops=0):
    moved = sum(a.size * a.dtype.itemsize for a in args)
    args = [
        pltpu.with_memory_space_constraint(a, pltpu.HBM) if spaces.get(i) is pltpu.HBM else a
        for i, a in enumerate(args)
    ]
    return pl.pallas_call(
        kernel,
        out_shape=[
            pltpu.SMEM(s, t) if out_spaces.get(i) is pltpu.SMEM else jax.ShapeDtypeStruct(s, t)
            for i, (s, t) in enumerate(outs)
        ],
        in_specs=[pl.BlockSpec(memory_space=spaces.get(i, pltpu.VMEM)) for i in range(len(args))],
        out_specs=[
            pl.BlockSpec(memory_space=out_spaces.get(i, pltpu.VMEM)) for i in range(len(outs))
        ],
        scratch_shapes=list(scratch),
        input_output_aliases=aliases,
        compiler_params=pltpu.CompilerParams(vmem_limit_bytes=VMEM_LIMIT),
        cost_estimate=pl.CostEstimate(flops=flops, bytes_accessed=moved, transcendentals=0),
        name=name,
    )(*args)


def prepare(x, q, first, leaves, lefts, loads):
    for leaf in range(leaves):
        here = slice(leaf * LEAF, (leaf + 1) * LEAF)
        lefts[first + leaf] = left_rows(x[:, here])
        loads[first + leaf] = q[:, here]


def own_kernel(x, q, lefts, loads):
    leaves = lefts.shape[0] // 3
    prepare(x, q, leaves, leaves, lefts, loads)


def halo_kernel(before_x, after_x, before_q, after_q, lefts_in, loads_in, lefts, loads):
    leaves = lefts.shape[0] // 3
    prepare(before_x, before_q, 0, leaves, lefts, loads)
    prepare(after_x, after_q, 2 * leaves, leaves, lefts, loads)


def near_part(start, count, shift, ids, lefts, rights, loads, out, held):
    turns = ids.shape[1]

    def fill(leaf, turn):
        source = ids[start + leaf, turn] - shift
        held[turn] = entries(lefts[source], rights[start + leaf]).astype(BF16)

    def use(leaf, turn, summed):
        source = ids[start + leaf, turn] - shift
        return summed + dot(loads[source], held[turn])

    for turn in range(turns):
        fill(0, turn)

    def step(leaf, carry):
        summed = jnp.zeros((NRHS, LEAF), F32)
        for turn in range(turns):
            summed = use(leaf - 1, turn, summed)
            fill(leaf, turn)
        out[leaf - 1] = summed
        return carry

    lax.fori_loop(1, count, step, 0)
    summed = jnp.zeros((NRHS, LEAF), F32)
    for turn in range(turns):
        summed = use(count - 1, turn, summed)
    out[count - 1] = summed


def beside(source, target_x, held, out):
    left = left_rows(source[0:DIM])
    right = right_rows(target_x)
    count = target_x.shape[1]
    for top in range(0, count, LEAF):
        for at in range(0, count, LEAF):
            held[top : top + LEAF, at : at + LEAF] = entries(
                left[top : top + LEAF], right[:, at : at + LEAF]
            ).astype(BF16)
    out[...] = dot(source[DIM:], held[...])


def near_kernel(start, count, ids, lefts, rights, loads, own, sibling, out, side, held, square):
    beside(sibling, own[0:DIM], square, side)
    shift = (lax.axis_index(("outer", "inner")) - 1) * rights.shape[0]
    near_part(start, count, shift, ids, lefts, rights, loads, out, held)


def link(parent_left, child_x, block, inverse):
    right = right_rows(child_x)
    count = child_x.shape[1]
    for at in range(0, count, LEAF):
        total = jnp.zeros((1, LEAF), F32)
        for top in range(0, count, LEAF):
            piece = entries(parent_left[top : top + LEAF], right[:, at : at + LEAF])
            total = total + jnp.sum(piece, axis=0, keepdims=True)
            block[top : top + LEAF, at : at + LEAF] = piece.astype(BF16)
        inverse[:, at : at + LEAF] = 1.0 / total


def lifted(charges, block, inverse):
    weights = (charges.astype(F32) * inverse[...]).astype(BF16)
    return dot_nt(weights, block[...])


def climb_kernel(level, tree, own, sibling, node, block, inverse, square, spare):
    next_x = pick(tiles_of(own[0:DIM]) + tiles_of(sibling[0:DIM]), tree[level : level + 1])
    left = left_rows(next_x)
    link(left, own[0:DIM], block, inverse)
    link(left, sibling[0:DIM], square, spare)
    up = lifted(own[DIM:], block, inverse) + lifted(sibling[DIM:], square, spare)
    node[0:DIM] = next_x.astype(BF16)
    node[DIM:] = up.astype(BF16)


def down_kernel(levels, own, sibling, *refs):
    blocks = refs[0 : 3 * levels]
    base_block, base_inverse = refs[3 * levels : 3 * levels + 2]
    nears = refs[3 * levels + 2 : -5]
    out, square, side, made, sems = refs[-5:]
    beside(sibling, own[0:DIM], square, side)
    downward = side[...].astype(BF16)
    for level in range(levels - 1, -1, -1):
        block, inverse, across = blocks[3 * level : 3 * level + 3]
        downward = (across[...] + dot(downward, block[...]) * inverse[...]).astype(BF16)
    at = 0
    writes = []
    for near in nears:
        first = at
        for leaf in range(near.shape[0]):
            here = slice(at, at + LEAF)
            made[:, here] = near[leaf] + dot(downward, base_block[:, here]) * base_inverse[:, here]
            at += LEAF
        here = slice(first, at)
        writes.append(
            pltpu.make_async_copy(made.at[:, here], out.at[:, here], sems.at[len(writes)])
        )
        writes[-1].start()
    for write in writes:
        write.wait()


def swapped(node, bit):
    total = lax.axis_size("inner") * lax.axis_size("outer")
    return lax.ppermute(node, ("outer", "inner"), [(i, i ^ (1 << bit)) for i in range(total)])


def body(points, charges, near_leaves, skel_device, skel_tree):
    ring = ("outer", "inner")
    total = lax.axis_size("inner") * lax.axis_size("outer")
    levels = total.bit_length() - 1
    width = points.shape[1]
    leaves, turns = near_leaves.shape
    count = skel_device.shape[1]
    tree = jnp.transpose(skel_tree, (1, 0, 2))
    ahead = [(i, (i + 1) % total) for i in range(total)]
    back = [((i + 1) % total, i) for i in range(total)]
    before_x = lax.ppermute(points, ring, ahead)
    after_x = lax.ppermute(points, ring, back)
    before_q = lax.ppermute(charges, ring, ahead)
    after_q = lax.ppermute(charges, ring, back)

    square = pltpu.VMEM((count, count), BF16)
    line = pltpu.VMEM((1, count), F32)
    side_out = ((NRHS, count), F32)
    node_out = ((DIM + NRHS, count), BF16)
    block_out = [((count, count), BF16), ((1, count), F32)]

    node, base_block, base_inverse, own_x, own_q, rights, tree, ids = call(
        base_kernel,
        [
            node_out,
            ((count, width), BF16),
            ((1, width), F32),
            (points.shape, BF16),
            (charges.shape, BF16),
            ((leaves, DEPTH, LEAF), BF16),
            ((tree.shape[0], count), jnp.int32),
            ((leaves, turns), jnp.int32),
        ],
        (points, charges, tree, skel_device, near_leaves),
        "base",
        [
            pltpu.VMEM(tree.shape, jnp.int32),
            pltpu.VMEM(skel_device.shape, jnp.int32),
            pltpu.SemaphoreType.DMA((5,)),
        ],
        spaces={i: pltpu.HBM for i in range(5)},
        out_spaces={7: pltpu.SMEM},
        flops=2 * width * count * (DEPTH + NRHS),
    )
    chunks = [0] + [leaves * (i + 1) // (levels - 1) - leaves * i // (levels - 1) for i in range(levels - 1)]
    sources_out = [((3 * leaves, LEAF, DEPTH), BF16), ((3 * leaves, NRHS, LEAF), BF16)]
    start = 0
    records = []
    nears = []
    pending = None
    for level in range(levels):
        sibling = swapped(node, level)
        if level == 0:
            own_x, node = lax.optimization_barrier((own_x, node))
            lefts, loads = call(own_kernel, sources_out, (own_x, own_q), "own", flops=10**8)
            lefts, sibling = lax.optimization_barrier((lefts, sibling))
        else:
            chunk = chunks[level]
            lefts, node = lax.optimization_barrier((lefts, node))
            if level == 1:
                lefts, loads = call(
                    halo_kernel,
                    sources_out,
                    (before_x, after_x, before_q, after_q, lefts, loads),
                    "halo",
                    aliases={4: 0, 5: 1},
                    flops=10**9,
                )
            part, side = call(
                functools.partial(near_kernel, start, chunk),
                [((chunk, NRHS, LEAF), F32), side_out],
                (ids, lefts, rights, loads, *pending),
                "near",
                [pltpu.VMEM((turns, LEAF, LEAF), BF16), square],
                spaces={0: pltpu.SMEM},
                flops=2 * chunk * LEAF * turns * LEAF * (DEPTH + NRHS),
            )
            start += chunk
            part, sibling = lax.optimization_barrier((part, sibling))
            nears.append(part)
            records[-1].append(side)
        if level < levels - 1:
            following, block, inverse = call(
                functools.partial(climb_kernel, level),
                [node_out, *block_out],
                (tree, node, sibling),
                "climb",
                [square, line],
                flops=2 * 2 * count * count * (DEPTH + NRHS),
            )
            records.append([block, inverse])
            pending = (node, sibling)
            node = following
    kept = [array for record in records for array in record]
    [potential] = call(
        functools.partial(down_kernel, levels - 1),
        [((NRHS, width), F32)],
        (node, sibling, *kept, base_block, base_inverse, *nears),
        "down",
        [
            square,
            pltpu.VMEM(*side_out),
            pltpu.VMEM((NRHS, width), F32),
            pltpu.SemaphoreType.DMA((len(nears),)),
        ],
        out_spaces={0: pl.ANY},
        flops=2 * width * count * NRHS,
    )
    return potential


def solution(mesh):
    return jax.shard_map(
        body,
        mesh=mesh,
        in_specs=(
            P(None, ("outer", "inner")),
            P(None, ("outer", "inner")),
            P(("outer", "inner"), None),
            P(("outer", "inner"), None),
            P(("outer", "inner"), None, None),
        ),
        out_specs=P(None, ("outer", "inner")),
        check_vma=False,
    )
```

```python
import functools
import math

import jax
import jax.numpy as jnp
from jax import lax
from jax.experimental import pallas as pl
from jax.experimental.pallas import tpu as pltpu
from jax.sharding import PartitionSpec as P

DIM = 16
NRHS = 64
LEAF = 256
TILE = 128
DEPTH = 32
GAMMA = 0.125
F32 = jnp.float32
BF16 = jnp.bfloat16

LOG2E = 1.0 / math.log(2.0)
VMEM_LIMIT = 24 * 2**20
REACH = (0, 0, 2, 0, 0, 0, 32, 16)


def split_rows(x):
    wide = x.astype(F32)
    rest = (-GAMMA) * jnp.sum(wide * wide, axis=0, keepdims=True)
    row = lax.broadcasted_iota(jnp.int32, (DIM, x.shape[1]), 0)
    terms = jnp.where((row >= 3) & (row < 6), 1.0, 0.0)
    for i in range(3):
        term = rest.astype(BF16).astype(F32)
        rest = rest - term
        terms = jnp.where(row == i, term, terms)
    return wide, row, terms


def left_rows(x):
    wide, row, terms = split_rows(x)
    return jnp.concatenate([wide, terms], 0).astype(BF16).T


def right_rows(x):
    wide, row, terms = split_rows(x)
    turned = jnp.where(row < 3, 1.0, 0.0)
    for i in range(3):
        turned = jnp.where(row == i + 3, terms[i : i + 1], turned)
    return jnp.concatenate([wide * (2.0 * GAMMA), turned], 0).astype(BF16)


def dot(a, b):
    return jnp.dot(a, b, preferred_element_type=F32)


def dot_nt(a, b):
    return lax.dot_general(a, b, (((1,), (1,)), ((), ())), preferred_element_type=F32)


def entries(left, right):
    return jnp.exp2(dot(left, right) * LOG2E)


def pick(tiles, index):
    out = []
    for at in range(0, index.shape[1], TILE):
        here = jnp.broadcast_to(index[:, at : at + TILE], (DIM, TILE))
        lane = here & (TILE - 1)
        which = here >> 7
        got = jnp.zeros((DIM, TILE), F32)
        for number, tile in enumerate(tiles):
            got = jnp.where(which == number, jnp.take_along_axis(tile, lane, axis=1), got)
        out.append(got)
    return jnp.concatenate(out, 1)


def tiles_of(x):
    x = x.astype(F32)
    return [x[:, at : at + TILE] for at in range(0, x.shape[1], TILE)]


def base_kernel(
    points_in, charges_in, tree_in, chosen_in, ids_in,
    node, block, inverse, points, charges, rights, tree_out, ids,
    tree, chosen, sems,
):
    position = lax.axis_index(("outer", "inner"))
    copies = [
        pltpu.make_async_copy(source, target, sems.at[i])
        for i, (source, target) in enumerate(
            (
                (points_in, points),
                (chosen_in, chosen),
                (tree_in, tree),
                (charges_in, charges),
                (ids_in, ids),
            )
        )
    ]
    for copy in copies:
        copy.start()
    leaves = rights.shape[0]
    copies[0].wait()
    copies[1].wait()
    base_x = pick(
        [points[:, at : at + TILE].astype(F32) for at in range(0, points.shape[1], TILE)],
        chosen[...],
    )
    node[0:DIM] = base_x.astype(BF16)
    left = left_rows(base_x)
    count = base_x.shape[1]
    copies[2].wait()
    for level in range(tree.shape[0]):
        bit = ((position >> level) & 1) * count
        tree_out[level : level + 1] = tree[level] ^ bit
    copies[3].wait()
    up = jnp.zeros((NRHS, count), F32)
    for leaf in range(leaves):
        here = slice(leaf * LEAF, (leaf + 1) * LEAF)
        right = right_rows(points[:, here])
        rights[leaf] = right
        total = jnp.zeros((1, LEAF), F32)
        for top in range(0, count, LEAF):
            piece = entries(left[top : top + LEAF], right)
            total = total + jnp.sum(piece, axis=0, keepdims=True)
            block[top : top + LEAF, here] = piece.astype(BF16)
        scale = 1.0 / total
        inverse[:, here] = scale
        weights = (charges[:, here].astype(F32) * scale).astype(BF16)
        up = up + dot_nt(weights, block[:, here])
    node[DIM:] = up.astype(BF16)
    copies[4].wait()


def call(kernel, outs, args, name, scratch=(), spaces={}, out_spaces={}, aliases={}, flops=0):
    moved = sum(a.size * a.dtype.itemsize for a in args)
    args = [
        pltpu.with_memory_space_constraint(a, pltpu.HBM) if spaces.get(i) is pltpu.HBM else a
        for i, a in enumerate(args)
    ]
    return pl.pallas_call(
        kernel,
        out_shape=[
            pltpu.SMEM(s, t) if out_spaces.get(i) is pltpu.SMEM else jax.ShapeDtypeStruct(s, t)
            for i, (s, t) in enumerate(outs)
        ],
        in_specs=[pl.BlockSpec(memory_space=spaces.get(i, pltpu.VMEM)) for i in range(len(args))],
        out_specs=[
            pl.BlockSpec(memory_space=out_spaces.get(i, pltpu.VMEM)) for i in range(len(outs))
        ],
        scratch_shapes=list(scratch),
        input_output_aliases=aliases,
        compiler_params=pltpu.CompilerParams(vmem_limit_bytes=VMEM_LIMIT),
        cost_estimate=pl.CostEstimate(flops=flops, bytes_accessed=moved, transcendentals=0),
        name=name,
    )(*args)


def prepare(x, q, first, leaves, lefts, loads):
    for leaf in range(leaves):
        here = slice(leaf * LEAF, (leaf + 1) * LEAF)
        lefts[first + leaf] = left_rows(x[:, here])
        loads[first + leaf] = q[:, here]


def own_kernel(x, q, lefts, loads):
    leaves = lefts.shape[0] // 3
    prepare(x, q, leaves, leaves, lefts, loads)


def halo_kernel(before_x, after_x, before_q, after_q, lefts_in, loads_in, lefts, loads):
    leaves = lefts.shape[0] // 3
    prepare(before_x, before_q, 0, leaves, lefts, loads)
    prepare(after_x, after_q, 2 * leaves, leaves, lefts, loads)


def near_part(start, count, shift, ids, lefts, rights, loads, out, held):
    turns = ids.shape[1]

    def fill(leaf, turn):
        source = ids[start + leaf, turn] - shift
        held[turn] = entries(lefts[source], rights[start + leaf]).astype(BF16)

    def use(leaf, turn, summed):
        source = ids[start + leaf, turn] - shift
        return summed + dot(loads[source], held[turn])

    for turn in range(turns):
        fill(0, turn)

    def step(leaf, carry):
        summed = jnp.zeros((NRHS, LEAF), F32)
        for turn in range(turns):
            summed = use(leaf - 1, turn, summed)
            fill(leaf, turn)
        out[leaf - 1] = summed
        return carry

    lax.fori_loop(1, count, step, 0)
    summed = jnp.zeros((NRHS, LEAF), F32)
    for turn in range(turns):
        summed = use(count - 1, turn, summed)
    out[count - 1] = summed


def beside(source, target_x, held, out):
    left = left_rows(source[0:DIM])
    right = right_rows(target_x)
    count = target_x.shape[1]
    for top in range(0, count, LEAF):
        for at in range(0, count, LEAF):
            held[top : top + LEAF, at : at + LEAF] = entries(
                left[top : top + LEAF], right[:, at : at + LEAF]
            ).astype(BF16)
    out[...] = dot(source[DIM:], held[...])


def near_kernel(start, count, ids, lefts, rights, loads, own, sibling, out, side, held, square):
    beside(sibling, own[0:DIM], square, side)
    shift = (lax.axis_index(("outer", "inner")) - 1) * rights.shape[0]
    near_part(start, count, shift, ids, lefts, rights, loads, out, held)


def link(parent_left, child_x, block, inverse):
    right = right_rows(child_x)
    count = child_x.shape[1]
    for at in range(0, count, LEAF):
        total = jnp.zeros((1, LEAF), F32)
        for top in range(0, count, LEAF):
            piece = entries(parent_left[top : top + LEAF], right[:, at : at + LEAF])
            total = total + jnp.sum(piece, axis=0, keepdims=True)
            block[top : top + LEAF, at : at + LEAF] = piece.astype(BF16)
        inverse[:, at : at + LEAF] = 1.0 / total


def lifted(charges, block, inverse):
    weights = (charges.astype(F32) * inverse[...]).astype(BF16)
    return dot_nt(weights, block[...])


def climb_kernel(level, tree, own, sibling, node, block, inverse, square, spare):
    next_x = pick(tiles_of(own[0:DIM]) + tiles_of(sibling[0:DIM]), tree[level : level + 1])
    left = left_rows(next_x)
    link(left, own[0:DIM], block, inverse)
    link(left, sibling[0:DIM], square, spare)
    up = lifted(own[DIM:], block, inverse) + lifted(sibling[DIM:], square, spare)
    node[0:DIM] = next_x.astype(BF16)
    node[DIM:] = up.astype(BF16)


def down_kernel(levels, own, sibling, *refs):
    blocks = refs[0 : 3 * levels]
    base_block, base_inverse = refs[3 * levels : 3 * levels + 2]
    nears = refs[3 * levels + 2 : -5]
    out, square, side, made, sems = refs[-5:]
    beside(sibling, own[0:DIM], square, side)
    downward = side[...].astype(BF16)
    for level in range(levels - 1, -1, -1):
        block, inverse, across = blocks[3 * level : 3 * level + 3]
        downward = (across[...] + dot(downward, block[...]) * inverse[...]).astype(BF16)
    at = 0
    writes = []
    for near in nears:
        first = at
        for leaf in range(near.shape[0]):
            here = slice(at, at + LEAF)
            made[:, here] = near[leaf] + dot(downward, base_block[:, here]) * base_inverse[:, here]
            at += LEAF
        here = slice(first, at)
        writes.append(
            pltpu.make_async_copy(made.at[:, here], out.at[:, here], sems.at[len(writes)])
        )
        writes[-1].start()
    for write in writes:
        write.wait()


def swapped(node, bit):
    total = lax.axis_size("inner") * lax.axis_size("outer")
    mask = (1 << bit) | (REACH[bit] if bit < len(REACH) else 0)
    return lax.ppermute(node, ("outer", "inner"), [(i, i ^ mask) for i in range(total)])


def body(points, charges, near_leaves, skel_device, skel_tree):
    ring = ("outer", "inner")
    total = lax.axis_size("inner") * lax.axis_size("outer")
    levels = total.bit_length() - 1
    width = points.shape[1]
    leaves, turns = near_leaves.shape
    count = skel_device.shape[1]
    tree = jnp.transpose(skel_tree, (1, 0, 2))
    ahead = [(i, (i + 1) % total) for i in range(total)]
    back = [((i + 1) % total, i) for i in range(total)]
    before_x = lax.ppermute(points, ring, ahead)
    after_x = lax.ppermute(points, ring, back)
    before_q = lax.ppermute(charges, ring, ahead)
    after_q = lax.ppermute(charges, ring, back)

    square = pltpu.VMEM((count, count), BF16)
    line = pltpu.VMEM((1, count), F32)
    side_out = ((NRHS, count), F32)
    node_out = ((DIM + NRHS, count), BF16)
    block_out = [((count, count), BF16), ((1, count), F32)]

    node, base_block, base_inverse, own_x, own_q, rights, tree, ids = call(
        base_kernel,
        [
            node_out,
            ((count, width), BF16),
            ((1, width), F32),
            (points.shape, BF16),
            (charges.shape, BF16),
            ((leaves, DEPTH, LEAF), BF16),
            ((tree.shape[0], count), jnp.int32),
            ((leaves, turns), jnp.int32),
        ],
        (points, charges, tree, skel_device, near_leaves),
        "base",
        [
            pltpu.VMEM(tree.shape, jnp.int32),
            pltpu.VMEM(skel_device.shape, jnp.int32),
            pltpu.SemaphoreType.DMA((5,)),
        ],
        spaces={i: pltpu.HBM for i in range(5)},
        out_spaces={7: pltpu.SMEM},
        flops=2 * width * count * (DEPTH + NRHS),
    )
    chunks = [0] + [leaves * (i + 1) // (levels - 1) - leaves * i // (levels - 1) for i in range(levels - 1)]
    sources_out = [((3 * leaves, LEAF, DEPTH), BF16), ((3 * leaves, NRHS, LEAF), BF16)]
    start = 0
    records = []
    nears = []
    pending = None
    for level in range(levels):
        sibling = swapped(node, level)
        if level == 0:
            own_x, node = lax.optimization_barrier((own_x, node))
            lefts, loads = call(own_kernel, sources_out, (own_x, own_q), "own", flops=10**8)
            lefts, sibling = lax.optimization_barrier((lefts, sibling))
        else:
            chunk = chunks[level]
            lefts, node = lax.optimization_barrier((lefts, node))
            if level == 1:
                lefts, loads = call(
                    halo_kernel,
                    sources_out,
                    (before_x, after_x, before_q, after_q, lefts, loads),
                    "halo",
                    aliases={4: 0, 5: 1},
                    flops=10**9,
                )
            part, side = call(
                functools.partial(near_kernel, start, chunk),
                [((chunk, NRHS, LEAF), F32), side_out],
                (ids, lefts, rights, loads, *pending),
                "near",
                [pltpu.VMEM((turns, LEAF, LEAF), BF16), square],
                spaces={0: pltpu.SMEM},
                flops=2 * chunk * LEAF * turns * LEAF * (DEPTH + NRHS),
            )
            start += chunk
            part, sibling = lax.optimization_barrier((part, sibling))
            nears.append(part)
            records[-1].append(side)
        if level < levels - 1:
            following, block, inverse = call(
                functools.partial(climb_kernel, level),
                [node_out, *block_out],
                (tree, node, sibling),
                "climb",
                [square, line],
                flops=2 * 2 * count * count * (DEPTH + NRHS),
            )
            records.append([block, inverse])
            pending = (node, sibling)
            node = following
    kept = [array for record in records for array in record]
    [potential] = call(
        functools.partial(down_kernel, levels - 1),
        [((NRHS, width), F32)],
        (node, sibling, *kept, base_block, base_inverse, *nears),
        "down",
        [
            square,
            pltpu.VMEM(*side_out),
            pltpu.VMEM((NRHS, width), F32),
            pltpu.SemaphoreType.DMA((len(nears),)),
        ],
        out_spaces={0: pl.ANY},
        flops=2 * width * count * NRHS,
    )
    return potential


def solution(mesh):
    return jax.shard_map(
        body,
        mesh=mesh,
        in_specs=(
            P(None, ("outer", "inner")),
            P(None, ("outer", "inner")),
            P(("outer", "inner"), None),
            P(("outer", "inner"), None),
            P(("outer", "inner"), None, None),
        ),
        out_specs=P(None, ("outer", "inner")),
        check_vma=False,
    )
```

```python
import functools
import math

import jax
import jax.numpy as jnp
from jax import lax
from jax.experimental import pallas as pl
from jax.experimental.pallas import tpu as pltpu
from jax.sharding import PartitionSpec as P

DIM = 16
NRHS = 64
LEAF = 256
TILE = 128
DEPTH = 32
GAMMA = 0.125
F32 = jnp.float32
BF16 = jnp.bfloat16

LOG2E = 1.0 / math.log(2.0)
VMEM_LIMIT = 24 * 2**20
REACH = (0, 0, 2, 0, 0, 0, 32, 16)


def split_rows(x):
    wide = x.astype(F32)
    rest = (-GAMMA) * jnp.sum(wide * wide, axis=0, keepdims=True)
    row = lax.broadcasted_iota(jnp.int32, (DIM, x.shape[1]), 0)
    terms = jnp.where((row >= 3) & (row < 6), 1.0, 0.0)
    for i in range(3):
        term = rest.astype(BF16).astype(F32)
        rest = rest - term
        terms = jnp.where(row == i, term, terms)
    return wide, row, terms


def left_rows(x):
    wide, row, terms = split_rows(x)
    return jnp.concatenate([wide, terms], 0).astype(BF16).T


def right_rows(x):
    wide, row, terms = split_rows(x)
    turned = jnp.where(row < 3, 1.0, 0.0)
    for i in range(3):
        turned = jnp.where(row == i + 3, terms[i : i + 1], turned)
    return jnp.concatenate([wide * (2.0 * GAMMA), turned], 0).astype(BF16)


def dot(a, b):
    return jnp.dot(a, b, preferred_element_type=F32)


def dot_nt(a, b):
    return lax.dot_general(a, b, (((1,), (1,)), ((), ())), preferred_element_type=F32)


def entries(left, right):
    return jnp.exp2(dot(left, right) * LOG2E)


def pick(tiles, index):
    out = []
    for at in range(0, index.shape[1], TILE):
        here = jnp.broadcast_to(index[:, at : at + TILE], (DIM, TILE))
        lane = here & (TILE - 1)
        which = here >> 7
        got = jnp.zeros((DIM, TILE), F32)
        for number, tile in enumerate(tiles):
            got = jnp.where(which == number, jnp.take_along_axis(tile, lane, axis=1), got)
        out.append(got)
    return jnp.concatenate(out, 1)


def tiles_of(x):
    x = x.astype(F32)
    return [x[:, at : at + TILE] for at in range(0, x.shape[1], TILE)]


def base_kernel(
    points_in, charges_in, tree_in, chosen_in, ids_in,
    node, block, inverse, points, charges, rights, tree_out, ids,
    tree, chosen, sems,
):
    position = lax.axis_index(("outer", "inner"))
    copies = [
        pltpu.make_async_copy(source, target, sems.at[i])
        for i, (source, target) in enumerate(
            (
                (points_in, points),
                (chosen_in, chosen),
                (tree_in, tree),
                (charges_in, charges),
                (ids_in, ids),
            )
        )
    ]
    for copy in copies:
        copy.start()
    leaves = rights.shape[0]
    copies[0].wait()
    copies[1].wait()
    base_x = pick(
        [points[:, at : at + TILE].astype(F32) for at in range(0, points.shape[1], TILE)],
        chosen[...],
    )
    node[0:DIM] = base_x.astype(BF16)
    left = left_rows(base_x)
    count = base_x.shape[1]
    copies[2].wait()
    for level in range(tree.shape[0]):
        bit = ((position >> level) & 1) * count
        tree_out[level : level + 1] = tree[level] ^ bit
    copies[3].wait()
    up = jnp.zeros((NRHS, count), F32)
    for leaf in range(leaves):
        here = slice(leaf * LEAF, (leaf + 1) * LEAF)
        right = right_rows(points[:, here])
        rights[leaf] = right
        total = jnp.zeros((1, LEAF), F32)
        for top in range(0, count, LEAF):
            piece = entries(left[top : top + LEAF], right)
            total = total + jnp.sum(piece, axis=0, keepdims=True)
            block[top : top + LEAF, here] = piece.astype(BF16)
        scale = 1.0 / total
        inverse[:, here] = scale
        weights = (charges[:, here].astype(F32) * scale).astype(BF16)
        up = up + dot_nt(weights, block[:, here])
    node[DIM:] = up.astype(BF16)
    copies[4].wait()


def call(kernel, outs, args, name, scratch=(), spaces={}, out_spaces={}, aliases={}, flops=0):
    moved = sum(a.size * a.dtype.itemsize for a in args)
    args = [
        pltpu.with_memory_space_constraint(a, pltpu.HBM) if spaces.get(i) is pltpu.HBM else a
        for i, a in enumerate(args)
    ]
    return pl.pallas_call(
        kernel,
        out_shape=[
            pltpu.SMEM(s, t) if out_spaces.get(i) is pltpu.SMEM else jax.ShapeDtypeStruct(s, t)
            for i, (s, t) in enumerate(outs)
        ],
        in_specs=[pl.BlockSpec(memory_space=spaces.get(i, pltpu.VMEM)) for i in range(len(args))],
        out_specs=[
            pl.BlockSpec(memory_space=out_spaces.get(i, pltpu.VMEM)) for i in range(len(outs))
        ],
        scratch_shapes=list(scratch),
        input_output_aliases=aliases,
        compiler_params=pltpu.CompilerParams(vmem_limit_bytes=VMEM_LIMIT),
        cost_estimate=pl.CostEstimate(flops=flops, bytes_accessed=moved, transcendentals=0),
        name=name,
    )(*args)


def prepare(x, q, first, leaves, lefts, loads):
    for leaf in range(leaves):
        here = slice(leaf * LEAF, (leaf + 1) * LEAF)
        lefts[first + leaf] = left_rows(x[:, here])
        loads[first + leaf] = q[:, here]


def own_kernel(x, q, lefts, loads):
    leaves = lefts.shape[0] // 3
    prepare(x, q, leaves, leaves, lefts, loads)


def halo_kernel(near_x, far_x, near_q, far_q, lefts_in, loads_in, lefts, loads):
    leaves = lefts.shape[0] // 3
    odd = lax.axis_index(("outer", "inner")) & 1
    prepare(near_x, near_q, 2 * leaves * (1 - odd), leaves, lefts, loads)
    prepare(far_x, far_q, 2 * leaves * odd, leaves, lefts, loads)


def near_part(start, count, shift, ids, lefts, rights, loads, out, held):
    turns = ids.shape[1]

    def fill(leaf, turn):
        source = ids[start + leaf, turn] - shift
        held[turn] = entries(lefts[source], rights[start + leaf]).astype(BF16)

    def use(leaf, turn, summed):
        source = ids[start + leaf, turn] - shift
        return summed + dot(loads[source], held[turn])

    for turn in range(turns):
        fill(0, turn)

    def step(leaf, carry):
        summed = jnp.zeros((NRHS, LEAF), F32)
        for turn in range(turns):
            summed = use(leaf - 1, turn, summed)
            fill(leaf, turn)
        out[leaf - 1] = summed
        return carry

    lax.fori_loop(1, count, step, 0)
    summed = jnp.zeros((NRHS, LEAF), F32)
    for turn in range(turns):
        summed = use(count - 1, turn, summed)
    out[count - 1] = summed


def beside(source, target_x, held, out):
    left = left_rows(source[0:DIM])
    right = right_rows(target_x)
    count = target_x.shape[1]
    for top in range(0, count, LEAF):
        for at in range(0, count, LEAF):
            held[top : top + LEAF, at : at + LEAF] = entries(
                left[top : top + LEAF], right[:, at : at + LEAF]
            ).astype(BF16)
    out[...] = dot(source[DIM:], held[...])


def near_kernel(start, count, ids, lefts, rights, loads, own, sibling, out, side, held, square):
    beside(sibling, own[0:DIM], square, side)
    shift = (lax.axis_index(("outer", "inner")) - 1) * rights.shape[0]
    near_part(start, count, shift, ids, lefts, rights, loads, out, held)


def link(parent_left, child_x, block, inverse):
    right = right_rows(child_x)
    count = child_x.shape[1]
    for at in range(0, count, LEAF):
        total = jnp.zeros((1, LEAF), F32)
        for top in range(0, count, LEAF):
            piece = entries(parent_left[top : top + LEAF], right[:, at : at + LEAF])
            total = total + jnp.sum(piece, axis=0, keepdims=True)
            block[top : top + LEAF, at : at + LEAF] = piece.astype(BF16)
        inverse[:, at : at + LEAF] = 1.0 / total


def lifted(charges, block, inverse):
    weights = (charges.astype(F32) * inverse[...]).astype(BF16)
    return dot_nt(weights, block[...])


def climb_kernel(level, tree, own, sibling, node, block, inverse, square, spare):
    next_x = pick(tiles_of(own[0:DIM]) + tiles_of(sibling[0:DIM]), tree[level : level + 1])
    left = left_rows(next_x)
    link(left, own[0:DIM], block, inverse)
    link(left, sibling[0:DIM], square, spare)
    up = lifted(own[DIM:], block, inverse) + lifted(sibling[DIM:], square, spare)
    node[0:DIM] = next_x.astype(BF16)
    node[DIM:] = up.astype(BF16)


def down_kernel(levels, own, sibling, *refs):
    blocks = refs[0 : 3 * levels]
    base_block, base_inverse = refs[3 * levels : 3 * levels + 2]
    nears = refs[3 * levels + 2 : -5]
    out, square, side, made, sems = refs[-5:]
    beside(sibling, own[0:DIM], square, side)
    downward = side[...].astype(BF16)
    for level in range(levels - 1, -1, -1):
        block, inverse, across = blocks[3 * level : 3 * level + 3]
        downward = (across[...] + dot(downward, block[...]) * inverse[...]).astype(BF16)
    at = 0
    writes = []
    for near in nears:
        first = at
        for leaf in range(near.shape[0]):
            here = slice(at, at + LEAF)
            made[:, here] = near[leaf] + dot(downward, base_block[:, here]) * base_inverse[:, here]
            at += LEAF
        here = slice(first, at)
        writes.append(
            pltpu.make_async_copy(made.at[:, here], out.at[:, here], sems.at[len(writes)])
        )
        writes[-1].start()
    for write in writes:
        write.wait()


def swapped(node, bit):
    total = lax.axis_size("inner") * lax.axis_size("outer")
    mask = (1 << bit) | (REACH[bit] if bit < len(REACH) else 0)
    return lax.ppermute(node, ("outer", "inner"), [(i, i ^ mask) for i in range(total)])


def body(points, charges, near_leaves, skel_device, skel_tree):
    ring = ("outer", "inner")
    total = lax.axis_size("inner") * lax.axis_size("outer")
    levels = total.bit_length() - 1
    width = points.shape[1]
    leaves, turns = near_leaves.shape
    count = skel_device.shape[1]
    tree = jnp.transpose(skel_tree, (1, 0, 2))
    near_pairs = [(i, i ^ 1) for i in range(total)]
    far_pairs = [(i, ((i + 1 ^ 1) - 1) % total) for i in range(total)]
    far_x = lax.ppermute(points, ring, far_pairs)
    far_q = lax.ppermute(charges, ring, far_pairs)
    near_x = lax.ppermute(points, ring, near_pairs)
    near_q = lax.ppermute(charges, ring, near_pairs)

    square = pltpu.VMEM((count, count), BF16)
    line = pltpu.VMEM((1, count), F32)
    side_out = ((NRHS, count), F32)
    node_out = ((DIM + NRHS, count), BF16)
    block_out = [((count, count), BF16), ((1, count), F32)]

    node, base_block, base_inverse, own_x, own_q, rights, tree, ids = call(
        base_kernel,
        [
            node_out,
            ((count, width), BF16),
            ((1, width), F32),
            (points.shape, BF16),
            (charges.shape, BF16),
            ((leaves, DEPTH, LEAF), BF16),
            ((tree.shape[0], count), jnp.int32),
            ((leaves, turns), jnp.int32),
        ],
        (points, charges, tree, skel_device, near_leaves),
        "base",
        [
            pltpu.VMEM(tree.shape, jnp.int32),
            pltpu.VMEM(skel_device.shape, jnp.int32),
            pltpu.SemaphoreType.DMA((5,)),
        ],
        spaces={i: pltpu.HBM for i in range(5)},
        out_spaces={7: pltpu.SMEM},
        flops=2 * width * count * (DEPTH + NRHS),
    )
    chunks = [0] + [leaves * (i + 1) // (levels - 1) - leaves * i // (levels - 1) for i in range(levels - 1)]
    sources_out = [((3 * leaves, LEAF, DEPTH), BF16), ((3 * leaves, NRHS, LEAF), BF16)]
    start = 0
    records = []
    nears = []
    pending = None
    for level in range(levels):
        sibling = swapped(node, level)
        if level == 0:
            own_x, node = lax.optimization_barrier((own_x, node))
            lefts, loads = call(own_kernel, sources_out, (own_x, own_q), "own", flops=10**8)
            lefts, sibling = lax.optimization_barrier((lefts, sibling))
        else:
            chunk = chunks[level]
            lefts, node = lax.optimization_barrier((lefts, node))
            if level == 1:
                lefts, loads = call(
                    halo_kernel,
                    sources_out,
                    (near_x, far_x, near_q, far_q, lefts, loads),
                    "halo",
                    aliases={4: 0, 5: 1},
                    flops=10**9,
                )
            part, side = call(
                functools.partial(near_kernel, start, chunk),
                [((chunk, NRHS, LEAF), F32), side_out],
                (ids, lefts, rights, loads, *pending),
                "near",
                [pltpu.VMEM((turns, LEAF, LEAF), BF16), square],
                spaces={0: pltpu.SMEM},
                flops=2 * chunk * LEAF * turns * LEAF * (DEPTH + NRHS),
            )
            start += chunk
            part, sibling = lax.optimization_barrier((part, sibling))
            nears.append(part)
            records[-1].append(side)
        if level < levels - 1:
            following, block, inverse = call(
                functools.partial(climb_kernel, level),
                [node_out, *block_out],
                (tree, node, sibling),
                "climb",
                [square, line],
                flops=2 * 2 * count * count * (DEPTH + NRHS),
            )
            records.append([block, inverse])
            pending = (node, sibling)
            node = following
    kept = [array for record in records for array in record]
    [potential] = call(
        functools.partial(down_kernel, levels - 1),
        [((NRHS, width), F32)],
        (node, sibling, *kept, base_block, base_inverse, *nears),
        "down",
        [
            square,
            pltpu.VMEM(*side_out),
            pltpu.VMEM((NRHS, width), F32),
            pltpu.SemaphoreType.DMA((len(nears),)),
        ],
        out_spaces={0: pl.ANY},
        flops=2 * width * count * NRHS,
    )
    return potential


def solution(mesh):
    return jax.shard_map(
        body,
        mesh=mesh,
        in_specs=(
            P(None, ("outer", "inner")),
            P(None, ("outer", "inner")),
            P(("outer", "inner"), None),
            P(("outer", "inner"), None),
            P(("outer", "inner"), None, None),
        ),
        out_specs=P(None, ("outer", "inner")),
        check_vma=False,
    )
```

```python
import functools
import math

import jax
import jax.numpy as jnp
from jax import lax
from jax.experimental import pallas as pl
from jax.experimental.pallas import tpu as pltpu
from jax.sharding import PartitionSpec as P

DIM = 16
NRHS = 64
LEAF = 256
TILE = 128
DEPTH = 32
GAMMA = 0.125
F32 = jnp.float32
BF16 = jnp.bfloat16

LOG2E = 1.0 / math.log(2.0)
VMEM_LIMIT = 24 * 2**20
REACH = (0, 0, 2, 0, 0, 0, 32, 16)


def split_rows(x):
    wide = x.astype(F32)
    rest = (-GAMMA) * jnp.sum(wide * wide, axis=0, keepdims=True)
    row = lax.broadcasted_iota(jnp.int32, (DIM, x.shape[1]), 0)
    terms = jnp.where((row >= 3) & (row < 6), 1.0, 0.0)
    for i in range(3):
        term = rest.astype(BF16).astype(F32)
        rest = rest - term
        terms = jnp.where(row == i, term, terms)
    return wide, row, terms


def left_rows(x):
    wide, row, terms = split_rows(x)
    return jnp.concatenate([wide, terms], 0).astype(BF16).T


def right_rows(x):
    wide, row, terms = split_rows(x)
    turned = jnp.where(row < 3, 1.0, 0.0)
    for i in range(3):
        turned = jnp.where(row == i + 3, terms[i : i + 1], turned)
    return jnp.concatenate([wide * (2.0 * GAMMA), turned], 0).astype(BF16)


def dot(a, b):
    return jnp.dot(a, b, preferred_element_type=F32)


def dot_nt(a, b):
    return lax.dot_general(a, b, (((1,), (1,)), ((), ())), preferred_element_type=F32)


def entries(left, right):
    return jnp.exp2(dot(left, right) * LOG2E)


def pick(tiles, index):
    out = []
    for at in range(0, index.shape[1], TILE):
        here = jnp.broadcast_to(index[:, at : at + TILE], (DIM, TILE))
        lane = here & (TILE - 1)
        which = here >> 7
        got = jnp.zeros((DIM, TILE), F32)
        for number, tile in enumerate(tiles):
            got = jnp.where(which == number, jnp.take_along_axis(tile, lane, axis=1), got)
        out.append(got)
    return jnp.concatenate(out, 1)


def tiles_of(x):
    x = x.astype(F32)
    return [x[:, at : at + TILE] for at in range(0, x.shape[1], TILE)]


def base_kernel(
    points_in, charges_in, tree_in, chosen_in, ids_in,
    node, block, inverse, points, charges, rights, tree_out, ids,
    tree, chosen, sems,
):
    position = lax.axis_index(("outer", "inner"))
    copies = [
        pltpu.make_async_copy(source, target, sems.at[i])
        for i, (source, target) in enumerate(
            (
                (points_in, points),
                (chosen_in, chosen),
                (tree_in, tree),
                (charges_in, charges),
                (ids_in, ids),
            )
        )
    ]
    for copy in copies:
        copy.start()
    leaves = rights.shape[0]
    copies[0].wait()
    copies[1].wait()
    base_x = pick(
        [points[:, at : at + TILE].astype(F32) for at in range(0, points.shape[1], TILE)],
        chosen[...],
    )
    node[0:DIM] = base_x.astype(BF16)
    left = left_rows(base_x)
    count = base_x.shape[1]
    copies[2].wait()
    for level in range(tree.shape[0]):
        bit = ((position >> level) & 1) * count
        tree_out[level : level + 1] = tree[level] ^ bit
    copies[3].wait()
    up = jnp.zeros((NRHS, count), F32)
    for leaf in range(leaves):
        here = slice(leaf * LEAF, (leaf + 1) * LEAF)
        right = right_rows(points[:, here])
        rights[leaf] = right
        total = jnp.zeros((1, LEAF), F32)
        for top in range(0, count, LEAF):
            piece = entries(left[top : top + LEAF], right)
            total = total + jnp.sum(piece, axis=0, keepdims=True)
            block[top : top + LEAF, here] = piece.astype(BF16)
        scale = 1.0 / total
        inverse[:, here] = scale
        weights = (charges[:, here].astype(F32) * scale).astype(BF16)
        up = up + dot_nt(weights, block[:, here])
    node[DIM:] = up.astype(BF16)
    copies[4].wait()


def call(kernel, outs, args, name, scratch=(), spaces={}, out_spaces={}, aliases={}, flops=0):
    moved = sum(a.size * a.dtype.itemsize for a in args)
    args = [
        pltpu.with_memory_space_constraint(a, pltpu.HBM) if spaces.get(i) is pltpu.HBM else a
        for i, a in enumerate(args)
    ]
    return pl.pallas_call(
        kernel,
        out_shape=[
            pltpu.SMEM(s, t) if out_spaces.get(i) is pltpu.SMEM else jax.ShapeDtypeStruct(s, t)
            for i, (s, t) in enumerate(outs)
        ],
        in_specs=[pl.BlockSpec(memory_space=spaces.get(i, pltpu.VMEM)) for i in range(len(args))],
        out_specs=[
            pl.BlockSpec(memory_space=out_spaces.get(i, pltpu.VMEM)) for i in range(len(outs))
        ],
        scratch_shapes=list(scratch),
        input_output_aliases=aliases,
        compiler_params=pltpu.CompilerParams(vmem_limit_bytes=VMEM_LIMIT),
        cost_estimate=pl.CostEstimate(flops=flops, bytes_accessed=moved, transcendentals=0),
        name=name,
    )(*args)


def prepare(x, q, first, leaves, lefts, loads):
    for leaf in range(leaves):
        here = slice(leaf * LEAF, (leaf + 1) * LEAF)
        lefts[first + leaf] = left_rows(x[:, here])
        loads[first + leaf] = q[:, here]


def own_kernel(x, q, lefts, loads):
    leaves = lefts.shape[0] // 3
    prepare(x, q, leaves, leaves, lefts, loads)


def halo_kernel(near_x, far_x, near_q, far_q, lefts_in, loads_in, lefts, loads):
    leaves = lefts.shape[0] // 3
    odd = lax.axis_index(("outer", "inner")) & 1
    prepare(near_x, near_q, 2 * leaves * (1 - odd), leaves, lefts, loads)
    prepare(far_x, far_q, 2 * leaves * odd, leaves, lefts, loads)


def near_part(start, count, shift, ids, lefts, rights, loads, out, held):
    turns = ids.shape[1]

    def fill(leaf, turn):
        source = ids[start + leaf, turn] - shift
        held[turn] = entries(lefts[source], rights[start + leaf]).astype(BF16)

    def use(leaf, turn, summed):
        source = ids[start + leaf, turn] - shift
        return summed + dot(loads[source], held[turn])

    for turn in range(turns):
        fill(0, turn)

    def step(leaf, carry):
        summed = jnp.zeros((NRHS, LEAF), F32)
        for turn in range(turns):
            summed = use(leaf - 1, turn, summed)
            fill(leaf, turn)
        out[leaf - 1] = summed
        return carry

    lax.fori_loop(1, count, step, 0)
    summed = jnp.zeros((NRHS, LEAF), F32)
    for turn in range(turns):
        summed = use(count - 1, turn, summed)
    out[count - 1] = summed


def beside(source, target_x, held, out):
    left = left_rows(source[0:DIM])
    right = right_rows(target_x)
    count = target_x.shape[1]
    for top in range(0, count, LEAF):
        for at in range(0, count, LEAF):
            held[top : top + LEAF, at : at + LEAF] = entries(
                left[top : top + LEAF], right[:, at : at + LEAF]
            ).astype(BF16)
    out[...] = dot(source[DIM : DIM + NRHS], held[...])


def near_kernel(start, count, ids, lefts, rights, loads, own, sibling, out, side, held, square):
    beside(sibling, own[0:DIM], square, side)
    shift = (lax.axis_index(("outer", "inner")) - 1) * rights.shape[0]
    near_part(start, count, shift, ids, lefts, rights, loads, out, held)


def link(parent_left, child_x, block, inverse):
    right = right_rows(child_x)
    count = child_x.shape[1]
    for at in range(0, count, LEAF):
        total = jnp.zeros((1, LEAF), F32)
        for top in range(0, count, LEAF):
            piece = entries(parent_left[top : top + LEAF], right[:, at : at + LEAF])
            total = total + jnp.sum(piece, axis=0, keepdims=True)
            block[top : top + LEAF, at : at + LEAF] = piece.astype(BF16)
        inverse[:, at : at + LEAF] = 1.0 / total


def lifted(charges, block, inverse):
    weights = (charges.astype(F32) * inverse[...]).astype(BF16)
    return dot_nt(weights, block[...])


def climb_kernel(level, tree, own, sibling, node, block, inverse, square, spare):
    next_x = pick(tiles_of(own[0:DIM]) + tiles_of(sibling[0:DIM]), tree[level : level + 1])
    left = left_rows(next_x)
    link(left, own[0:DIM], block, inverse)
    link(left, sibling[0:DIM], square, spare)
    up = lifted(own[DIM : DIM + NRHS], block, inverse) + lifted(
        sibling[DIM : DIM + NRHS], square, spare
    )
    node[0:DIM] = next_x.astype(BF16)
    node[DIM : DIM + NRHS] = up.astype(BF16)
    if node.shape[0] > DIM + NRHS:
        index = tree[level + 1 : level + 2]
        row = lax.broadcasted_iota(jnp.int32, (16, index.shape[1]), 0)
        high = (index >> 5).astype(F32)
        low = (index & 31).astype(F32)
        node[DIM + NRHS :] = jnp.where(row == 0, high, jnp.where(row == 1, low, 0.0)).astype(BF16)


def down_kernel(levels, tree, own, sibling, cousin, far_cousin, *refs):
    blocks = refs[0 : 3 * levels]
    base_block, base_inverse = refs[3 * levels : 3 * levels + 2]
    nears = refs[3 * levels + 2 : -9]
    out, square, side, made, sems, spare, top_block, top_inverse, uncle = refs[-9:]
    parent_x = pick(tiles_of(own[0:DIM]) + tiles_of(sibling[0:DIM]), tree[levels : levels + 1])
    digits = cousin[DIM + NRHS :].astype(F32)
    uncle_x = pick(
        tiles_of(cousin[0:DIM]) + tiles_of(far_cousin[0:DIM]),
        (digits[0:1] * 32.0 + digits[1:2]).astype(jnp.int32),
    )
    link(left_rows(parent_x), own[0:DIM], top_block, top_inverse)
    left = left_rows(uncle_x)
    link(left, cousin[0:DIM], square, spare)
    up = lifted(cousin[DIM : DIM + NRHS], square, spare)
    link(left, far_cousin[0:DIM], square, spare)
    up = up + lifted(far_cousin[DIM : DIM + NRHS], square, spare)
    uncle[0:DIM] = uncle_x.astype(BF16)
    uncle[DIM:] = up.astype(BF16)
    beside(uncle, parent_x, square, side)
    downward = side[...].astype(BF16)
    beside(sibling, own[0:DIM], square, side)
    downward = (side[...] + dot(downward, top_block[...]) * top_inverse[...]).astype(BF16)
    for level in range(levels - 1, -1, -1):
        block, inverse, across = blocks[3 * level : 3 * level + 3]
        downward = (across[...] + dot(downward, block[...]) * inverse[...]).astype(BF16)
    at = 0
    writes = []
    for near in nears:
        first = at
        for leaf in range(near.shape[0]):
            here = slice(at, at + LEAF)
            made[:, here] = near[leaf] + dot(downward, base_block[:, here]) * base_inverse[:, here]
            at += LEAF
        here = slice(first, at)
        writes.append(
            pltpu.make_async_copy(made.at[:, here], out.at[:, here], sems.at[len(writes)])
        )
        writes[-1].start()
    for write in writes:
        write.wait()


def swapped(node, *bits):
    total = lax.axis_size("inner") * lax.axis_size("outer")
    mask = 0
    for bit in bits:
        mask |= (1 << bit) | (REACH[bit] if bit < len(REACH) else 0)
    return lax.ppermute(node, ("outer", "inner"), [(i, i ^ mask) for i in range(total)])


def body(points, charges, near_leaves, skel_device, skel_tree):
    ring = ("outer", "inner")
    total = lax.axis_size("inner") * lax.axis_size("outer")
    levels = total.bit_length() - 1
    width = points.shape[1]
    leaves, turns = near_leaves.shape
    count = skel_device.shape[1]
    tree = jnp.transpose(skel_tree, (1, 0, 2))
    near_pairs = [(i, i ^ 1) for i in range(total)]
    far_pairs = [(i, ((i + 1 ^ 1) - 1) % total) for i in range(total)]
    far_x = lax.ppermute(points, ring, far_pairs)
    far_q = lax.ppermute(charges, ring, far_pairs)
    near_x = lax.ppermute(points, ring, near_pairs)
    near_q = lax.ppermute(charges, ring, near_pairs)

    square = pltpu.VMEM((count, count), BF16)
    line = pltpu.VMEM((1, count), F32)
    side_out = ((NRHS, count), F32)
    node_out = ((DIM + NRHS, count), BF16)
    block_out = [((count, count), BF16), ((1, count), F32)]

    node, base_block, base_inverse, own_x, own_q, rights, tree, ids = call(
        base_kernel,
        [
            node_out,
            ((count, width), BF16),
            ((1, width), F32),
            (points.shape, BF16),
            (charges.shape, BF16),
            ((leaves, DEPTH, LEAF), BF16),
            ((tree.shape[0], count), jnp.int32),
            ((leaves, turns), jnp.int32),
        ],
        (points, charges, tree, skel_device, near_leaves),
        "base",
        [
            pltpu.VMEM(tree.shape, jnp.int32),
            pltpu.VMEM(skel_device.shape, jnp.int32),
            pltpu.SemaphoreType.DMA((5,)),
        ],
        spaces={i: pltpu.HBM for i in range(5)},
        out_spaces={7: pltpu.SMEM},
        flops=2 * width * count * (DEPTH + NRHS),
    )
    rest = levels - 3
    chunks = [0] + [2 + (i == 3) for i in range(rest)]
    chunks.append(leaves - sum(chunks))
    sources_out = [((3 * leaves, LEAF, DEPTH), BF16), ((3 * leaves, NRHS, LEAF), BF16)]
    start = 0
    records = []
    nears = []
    pending = None
    for level in range(levels - 1):
        last = level == levels - 2
        sibling = swapped(node, level)
        if last:
            cousin = swapped(node, level + 1)
            far_cousin = swapped(node, level, level + 1)
        if level == 0:
            own_x, node = lax.optimization_barrier((own_x, node))
            lefts, loads = call(own_kernel, sources_out, (own_x, own_q), "own", flops=10**8)
            lefts, sibling = lax.optimization_barrier((lefts, sibling))
        else:
            chunk = chunks[level]
            lefts, node = lax.optimization_barrier((lefts, node))
            if level == 1:
                lefts, loads = call(
                    halo_kernel,
                    sources_out,
                    (near_x, far_x, near_q, far_q, lefts, loads),
                    "halo",
                    aliases={4: 0, 5: 1},
                    flops=10**9,
                )
            part, side = call(
                functools.partial(near_kernel, start, chunk),
                [((chunk, NRHS, LEAF), F32), side_out],
                (ids, lefts, rights, loads, *pending),
                "near",
                [pltpu.VMEM((turns, LEAF, LEAF), BF16), square],
                spaces={0: pltpu.SMEM},
                flops=2 * chunk * LEAF * turns * LEAF * (DEPTH + NRHS),
            )
            start += chunk
            if last:
                part, cousin, far_cousin = lax.optimization_barrier((part, cousin, far_cousin))
            part, sibling = lax.optimization_barrier((part, sibling))
            nears.append(part)
            records[-1].append(side)
        if not last:
            extra = 16 if level == levels - 3 else 0
            following, block, inverse = call(
                functools.partial(climb_kernel, level),
                [((DIM + NRHS + extra, count), BF16), *block_out],
                (tree, node, sibling),
                "climb",
                [square, line],
                flops=2 * 2 * count * count * (DEPTH + NRHS),
            )
            records.append([block, inverse])
            pending = (node, sibling)
            node = following
    kept = [array for record in records for array in record]
    [potential] = call(
        functools.partial(down_kernel, levels - 2),
        [((NRHS, width), F32)],
        (tree, node, sibling, cousin, far_cousin, *kept, base_block, base_inverse, *nears),
        "down",
        [
            square,
            pltpu.VMEM(*side_out),
            pltpu.VMEM((NRHS, width), F32),
            pltpu.SemaphoreType.DMA((len(nears),)),
            line,
            square,
            line,
            pltpu.VMEM(*node_out),
        ],
        out_spaces={0: pl.ANY},
        flops=2 * width * count * NRHS,
    )
    return potential


def solution(mesh):
    return jax.shard_map(
        body,
        mesh=mesh,
        in_specs=(
            P(None, ("outer", "inner")),
            P(None, ("outer", "inner")),
            P(("outer", "inner"), None),
            P(("outer", "inner"), None),
            P(("outer", "inner"), None, None),
        ),
        out_specs=P(None, ("outer", "inner")),
        check_vma=False,
    )
```
